32 devices in a mesh: row: 4 (over z), col: 8 (over y, x, core).
Axes of the slice: x: 2, y: 2, z: 4, core: 2. Of those that a mesh axis runs over, the one named last changes fastest.
Arguments:
- scalars: float32 [1, 256, 256, 512], P(None, 'row', 'col'), may hold values from -6 to 6
- velocity: bfloat16 [3, 256, 256, 512], P(None, 'row', 'col'), may hold values from -6 to 6
- first_x: bfloat16 [512, 512], replicated, may hold values from -0.25 to 0.25
- second_x: bfloat16 [512, 512], replicated, may hold values from -0.25 to 0.25
- first_y: bfloat16 [256, 256], replicated, may hold values from -0.375 to 0.375
- second_y: bfloat16 [256, 256], replicated, may hold values from -0.375 to 0.375
- first_z: bfloat16 [256, 256], replicated, may hold values from -0.375 to 0.375
- second_z: bfloat16 [256, 256], replicated, may hold values from -0.375 to 0.375
Outputs:
- updated: float32 [1, 256, 256, 512], P(None, 'row', 'col')
The draws below stay inside these ranges and needn't reach their ends.
All inputs are finite; a program needn't handle non-finite values.
Results may differ from the reference program's by a relative error of at most 0.0021.
Values may be sent and summed in bfloat16 or wider, within the bound.
A program may use at most 128 MiB of HBM per device.

```python
import jax
import jax.numpy as jnp
from jax import lax

NX = 512
NY = 256
NZ = 256
NS = 1


def levels(key, extent, pieces, smallest, largest):
    gain, own = 1.0, jax.random.fold_in(key, 6)
    for axis_at, shards_of in pieces:
        draws = jnp.exp(jax.random.uniform(jax.random.fold_in(own, axis_at), (shards_of,), jnp.float32, smallest / len(pieces), largest / len(pieces)))
        gain = gain * jnp.repeat(draws, extent[axis_at] // shards_of).reshape([-1 if axis == axis_at else 1 for axis in range(len(extent))])
    return gain


def centred(stream_key, extent, spread, reach, shards=(), dtype=jnp.bfloat16):
    entries = jax.random.normal(stream_key, extent, jnp.float32) * spread
    if len(shards) > 0:
        entries = levels(stream_key, extent, shards, -0.22, 0.18) * entries
    return jnp.clip(entries, min=-reach, max=reach).astype(dtype)


def setup_inputs(seed: int = 0) -> dict:
    keys = jax.random.split(jax.random.key(seed), 9)
    scalars = centred(keys[0], (NS, NY, NZ, NX), 1.0, 6.0, ((1, 4), (2, 8)), jnp.float32)
    velocity = centred(keys[1], (3, NY, NZ, NX), 1.0, 6.0, ((1, 4), (2, 8)))
    first_x = centred(keys[2], (NX, NX), NX ** -0.5, 0.25)
    second_x = centred(keys[3], (NX, NX), NX ** -0.5, 0.25)
    first_y = centred(keys[4], (NY, NY), NY ** -0.5, 0.375)
    second_y = centred(keys[5], (NY, NY), NY ** -0.5, 0.375)
    first_z = centred(keys[6], (NZ, NZ), NZ ** -0.5, 0.375)
    second_z = centred(keys[7], (NZ, NZ), NZ ** -0.5, 0.375)
    return {"scalars": scalars, "velocity": velocity, "first_x": first_x, "second_x": second_x, "first_y": first_y, "second_y": second_y, "first_z": first_z, "second_z": second_z}


diffusion_coefficient = 0.5
step_weight = 0.5


def apply_along(scalar_values, matrix, spatial_axis):
    shifted = jnp.moveaxis(scalar_values, spatial_axis, -1)
    result = jnp.dot(shifted, matrix.T, preferred_element_type=jnp.float32)
    return jnp.moveaxis(result, -1, spatial_axis)


def one_scalar(scalar_values, velocity, first_x, second_x, first_y, second_y, first_z, second_z):
    compiled_step = scalar_values.astype(jnp.bfloat16)
    tendency_sum = jnp.zeros_like(scalar_values)
    solver_options = ((velocity[0], first_x, second_x, 2), (velocity[1], first_y, second_y, 0), (velocity[2], first_z, second_z, 1))
    for velocity_field, first_derivative_matrix, second_derivative_matrix, spatial_axis in solver_options:
        velocity_flux = velocity_field.astype(jnp.float32)
        flux_product = (velocity_flux * compiled_step.astype(jnp.float32)).astype(jnp.bfloat16)
        scalar_gradient = apply_along(compiled_step, first_derivative_matrix, spatial_axis)
        advected_scalar = apply_along(flux_product, first_derivative_matrix, spatial_axis)
        second_derivative = apply_along(compiled_step, second_derivative_matrix, spatial_axis)
        tendency_sum = tendency_sum + (-0.5 * (velocity_flux * scalar_gradient + advected_scalar) + diffusion_coefficient * second_derivative)
    return scalar_values + step_weight * tendency_sum


def reference(scalars, velocity, first_x, second_x, first_y, second_y, first_z, second_z):
    return lax.map(lambda scalar_values: one_scalar(scalar_values, velocity, first_x, second_x, first_y, second_y, first_z, second_z), scalars)
```

```python
import functools

import jax
import jax.numpy as jnp
from jax import lax
from jax.experimental import pallas as pl
from jax.experimental.pallas import tpu as pltpu
from jax.sharding import PartitionSpec as P

diffusion_coefficient = 0.5
step_weight = 0.5
MESH = pl.DeviceIdType.MESH
LANES = 128

Y_CHUNKS = 4
Z_CHUNKS = 2


def contract_last(scalar_values, matrix):
    return lax.dot_general(
        scalar_values,
        matrix,
        (((scalar_values.ndim - 1,), (1,)), ((), ())),
        preferred_element_type=jnp.float32,
    )


def contract_middle(scalar_values, matrix):
    return jnp.einsum("syc,ky->skc", scalar_values, matrix, preferred_element_type=jnp.float32)


def derivative_pair(scalar_values, first_derivative_matrix, second_derivative_matrix, apply_matrix):
    return (
        apply_matrix(scalar_values, first_derivative_matrix),
        apply_matrix(scalar_values, second_derivative_matrix),
    )


def axis_contribution(
    scalar_values, velocity_field, first_derivative_matrix, second_derivative_matrix, apply_matrix
):
    velocity_flux = velocity_field.astype(jnp.float32)
    flux_product = (velocity_flux * scalar_values.astype(jnp.float32)).astype(jnp.bfloat16)
    scalar_gradient, second_derivative = derivative_pair(
        scalar_values, first_derivative_matrix, second_derivative_matrix, apply_matrix
    )
    advected_scalar = apply_matrix(flux_product, first_derivative_matrix)
    return (
        -0.5 * (velocity_flux * scalar_gradient + advected_scalar)
        + diffusion_coefficient * second_derivative
    )


def body(scalars, velocity, first_x, second_x, first_y, second_y, first_z, second_z):
    scalar_count = scalars.shape[0]
    rows_local = scalars.shape[1]
    depth_z = scalars.shape[2]
    length_x = scalars.shape[3]
    compiled_step = scalars.astype(jnp.bfloat16)
    x_term = axis_contribution(compiled_step, velocity[0], first_x, second_x, contract_last)
    turned = jnp.transpose(jnp.concatenate([compiled_step, velocity[1:]], axis=0), (0, 1, 3, 2))
    y_payload = turned[: scalar_count + 1].reshape(scalar_count + 1, rows_local, length_x * depth_z)
    z_payload = jnp.concatenate([turned[:scalar_count], turned[scalar_count + 1 :]], axis=0)
    pencil_y = lax.all_to_all(y_payload, "row", split_axis=2, concat_axis=1, tiled=True)
    pencil_z = lax.all_to_all(z_payload, "col", split_axis=2, concat_axis=3, tiled=True)
    y_term = axis_contribution(
        pencil_y[:scalar_count], pencil_y[scalar_count], first_y, second_y, contract_middle
    )
    z_term = axis_contribution(
        pencil_z[:scalar_count], pencil_z[scalar_count], first_z, second_z, contract_last
    )
    y_home = lax.all_to_all(y_term, "row", split_axis=1, concat_axis=2, tiled=True)
    z_home = lax.all_to_all(z_term, "col", split_axis=3, concat_axis=2, tiled=True)
    returned = y_home.reshape(scalar_count, rows_local, length_x, depth_z) + z_home
    returned = jnp.transpose(returned, (0, 1, 3, 2))
    return scalars + step_weight * (x_term + returned)


def pair_term(velocity, gradient, advected, second):
    half = 0.5 * step_weight
    return -half * (velocity * gradient + advected) + (step_weight * diffusion_coefficient) * second


def dot(a, b):
    return jnp.dot(a, b, preferred_element_type=jnp.float32)


def dot_rows(a, b):
    return lax.dot_general(a, b, (((1,), (1,)), ((), ())), preferred_element_type=jnp.float32)


def kernel(
    rows, cols, scal, vel, f1x, f2x, f1y, f2y, f1z, f2z, out,
    acc, vb, vf, turned, py, ysend, yhome, sw, ub, pz, zsend, zhome,
    m1x, m2x, m1y, m2y, m1z, m2z,
    in_sem, own_sem, yf_send, yf_recv, yr_send, yr_recv, zf_send, zf_recv, zr_send, zr_recv,
):
    my_row, my_col = lax.axis_index("row"), lax.axis_index("col")
    ylen, zlen, xlen = ub.shape
    blocks = xlen // LANES
    zc = zlen // Y_CHUNKS
    yb = ylen // cols
    yc = yb // Z_CHUNKS

    def row_of(d):
        return lax.rem(my_row + d, rows)

    def col_of(d):
        return lax.rem(my_col + d, cols)

    def lanes(b):
        return pl.ds(b * LANES, LANES)

    loads = []

    def load(src, dst):
        copy = pltpu.make_async_copy(src, dst, in_sem.at[len(loads)])
        copy.start()
        loads.append(copy)
        return copy

    scal_in = [load(scal.at[:, lanes(b)], acc.at[b]) for b in range(blocks)]
    v_in = [load(vel.at[1, :, :, lanes(b)], vb.at[b]) for b in range(blocks)]
    w_in = load(vel.at[2], sw.at[:, 1])
    u_in = load(vel.at[0], ub)
    x_in = [load(f1x, m1x), load(f2x, m2x)]
    y_in = [load(f1y, m1y), load(f2y, m2y)]
    z_in = [load(f1z, m1z), load(f2z, m2z)]

    barrier = pltpu.get_barrier_semaphore()
    for d in range(1, rows):
        pl.semaphore_signal(barrier, inc=1, device_id=(row_of(d), my_col), device_id_type=MESH)
    for d in range(1, cols):
        pl.semaphore_signal(barrier, inc=1, device_id=(my_row, col_of(d)), device_id_type=MESH)

    def y_forward(k, d, sender, receiver):
        zs = pl.ds(k * zc, zc)
        return pltpu.make_async_remote_copy(
            src_ref=turned.at[receiver, zs],
            dst_ref=py.at[zs, :, pl.ds(sender * ylen, ylen)],
            send_sem=yf_send.at[k, d - 1], recv_sem=yf_recv.at[k, d - 1],
            device_id=(row_of(d), my_col), device_id_type=MESH)

    def y_return(k, d, sender, receiver):
        zs = pl.ds(k * zc, zc)
        return pltpu.make_async_remote_copy(
            src_ref=ysend.at[zs, pl.ds(receiver * ylen, ylen)],
            dst_ref=yhome.at[sender, zs],
            send_sem=yr_send.at[k, d - 1], recv_sem=yr_recv.at[k, d - 1],
            device_id=(row_of(d), my_col), device_id_type=MESH)

    def z_forward(k, d, sender, receiver):
        return pltpu.make_async_remote_copy(
            src_ref=sw.at[pl.ds(receiver * yb + k * yc, yc)],
            dst_ref=pz.at[pl.ds(k * yc, yc), :, pl.ds(sender * zlen, zlen)],
            send_sem=zf_send.at[k, d - 1], recv_sem=zf_recv.at[k, d - 1],
            device_id=(my_row, col_of(d)), device_id_type=MESH)

    def z_return(k, d, sender, receiver):
        return pltpu.make_async_remote_copy(
            src_ref=zsend.at[pl.ds(k * yc, yc), pl.ds(receiver * zlen, zlen)],
            dst_ref=zhome.at[pl.ds(sender * yb + k * yc, yc)],
            send_sem=zr_send.at[k, d - 1], recv_sem=zr_recv.at[k, d - 1],
            device_id=(my_row, col_of(d)), device_id_type=MESH)

    def own_copy(src, dst, index):
        copy = pltpu.make_async_copy(src, dst, own_sem.at[index])
        copy.start()
        return copy

    for copy in scal_in + v_in:
        copy.wait()

    @pl.loop(0, ylen)
    def _(y):
        span = pl.ds(pl.multiple_of(y * zlen, zlen), zlen)
        for b in range(blocks):
            vf[b, span] = vb[b, y].astype(jnp.float32)

    own = {}
    sends = []

    def order(n):
        return range(n - 1, 0, -1)

    def turn_and_send_y(k):
        @pl.loop(k * zc, (k + 1) * zc)
        def _(z):
            for b in range(blocks):
                turned[b, z, 0] = acc[b, pl.ds(z, ylen, stride=zlen), :].astype(jnp.bfloat16)
                turned[b, z, 1] = vf[b, pl.ds(z, ylen, stride=zlen), :].astype(jnp.bfloat16)

        if k == 0:
            pl.semaphore_wait(barrier, rows + cols - 2)
        for d in order(rows):
            copy = y_forward(k, d, my_row, row_of(d))
            copy.start()
            sends.append(copy)
        zs = pl.ds(k * zc, zc)
        own["yf", k] = own_copy(
            turned.at[my_row, zs], py.at[zs, :, pl.ds(my_row * ylen, ylen)], k)

    turn_and_send_y(0)

    @pl.loop(0, ylen)
    def _(y):
        span = pl.ds(pl.multiple_of(y * zlen, zlen), zlen)
        for b in range(blocks):
            sw[y, 0, :, lanes(b)] = acc[b, span].astype(jnp.bfloat16)

    w_in.wait()
    for k in range(Z_CHUNKS):
        for d in order(cols):
            copy = z_forward(k, d, my_col, col_of(d))
            copy.start()
            sends.append(copy)
        own["zf", k] = own_copy(
            sw.at[pl.ds(my_col * yb + k * yc, yc)],
            pz.at[pl.ds(k * yc, yc), :, pl.ds(my_col * zlen, zlen)], Y_CHUNKS + k)
    for k in range(1, Y_CHUNKS):
        turn_and_send_y(k)

    u_in.wait()
    for copy in x_in:
        copy.wait()
    y_tile = max(1, 256 // zlen)
    while ylen % y_tile:
        y_tile -= 1
    tile = y_tile * zlen

    @pl.loop(0, ylen // y_tile)
    def _(i):
        ys = pl.ds(i * y_tile, y_tile)
        span = pl.ds(pl.multiple_of(i * tile, tile), tile)
        s = sw[ys, 0].reshape(tile, xlen)
        u = ub[ys].reshape(tile, xlen).astype(jnp.float32)
        flux = (u * s.astype(jnp.float32)).astype(jnp.bfloat16)
        term = pair_term(u, dot_rows(s, m1x[...]), dot_rows(flux, m1x[...]), dot_rows(s, m2x[...]))
        for b in range(blocks):
            acc[b, span] += term[:, b * LANES:(b + 1) * LANES]

    for copy in y_in + z_in:
        copy.wait()

    def y_terms(k):
        own["yf", k].wait()
        for d in order(rows):
            y_forward(k, d, row_of(rows - d), my_row).wait_recv()

        @pl.loop(k * zc, (k + 1) * zc)
        def _(z):
            s = py[z, 0]
            v = py[z, 1].astype(jnp.float32)
            flux = (v * s.astype(jnp.float32)).astype(jnp.bfloat16)
            both = dot(m1y[...], jnp.concatenate([s, flux], axis=1))
            term = pair_term(v, both[:, :LANES], both[:, LANES:], dot(m2y[...], s))
            ysend[z] = term.astype(jnp.bfloat16)

        for d in order(rows):
            copy = y_return(k, d, my_row, row_of(d))
            copy.start()
            sends.append(copy)
        zs = pl.ds(k * zc, zc)
        own["yr", k] = own_copy(
            ysend.at[zs, pl.ds(my_row * ylen, ylen)], yhome.at[my_row, zs],
            Y_CHUNKS + Z_CHUNKS + k)

    def z_terms(k):
        own["zf", k].wait()
        for d in order(cols):
            z_forward(k, d, col_of(cols - d), my_col).wait_recv()

        @pl.loop(k * yc, (k + 1) * yc)
        def _(y):
            s = pz[y, 0]
            w = pz[y, 1].astype(jnp.float32)
            flux = (w * s.astype(jnp.float32)).astype(jnp.bfloat16)
            term = pair_term(w, dot(m1z[...], s), dot(m1z[...], flux), dot(m2z[...], s))
            zsend[y] = term.astype(jnp.bfloat16)

        for d in order(cols):
            copy = z_return(k, d, my_col, col_of(d))
            copy.start()
            sends.append(copy)
        own["zr", k] = own_copy(
            zsend.at[pl.ds(k * yc, yc), pl.ds(my_col * zlen, zlen)],
            zhome.at[pl.ds(my_col * yb + k * yc, yc)],
            2 * Y_CHUNKS + Z_CHUNKS + k)

    y_terms(0)
    for k in range(Z_CHUNKS):
        z_terms(k)
    for k in range(1, Y_CHUNKS):
        y_terms(k)

    for k in range(Z_CHUNKS):
        own["zr", k].wait()
        for d in order(cols):
            z_return(k, d, col_of(cols - d), my_col).wait_recv()

    @pl.loop(0, ylen)
    def _(y):
        span = pl.ds(pl.multiple_of(y * zlen, zlen), zlen)
        for b in range(blocks):
            acc[b, span] += zhome[y, :, lanes(b)].astype(jnp.float32)

    for k in range(Y_CHUNKS):
        own["yr", k].wait()
        for d in order(rows):
            y_return(k, d, row_of(rows - d), my_row).wait_recv()

        @pl.loop(k * zc, (k + 1) * zc)
        def _(z):
            for b in range(blocks):
                span = pl.ds(z, ylen, stride=zlen)
                acc[b, span, :] = acc[b, span, :] + yhome[b, z].astype(jnp.float32)

    stores = []
    for b in range(blocks):
        copy = pltpu.make_async_copy(acc.at[b], out.at[:, lanes(b)], in_sem.at[b])
        copy.start()
        stores.append(copy)
    for copy in sends:
        copy.wait_send()
    for copy in stores:
        copy.wait()


def fused(rows, cols, scalars, velocity, *matrices):
    _, ylen, zlen, xlen = scalars.shape
    blocks = xlen // LANES
    points = ylen * zlen
    yb = ylen // cols
    bf, f32 = jnp.bfloat16, jnp.float32
    sems = pltpu.SemaphoreType.DMA
    flops = 6 * points * xlen * (xlen + ylen * rows + zlen * cols)
    result = pl.pallas_call(
        functools.partial(kernel, rows, cols),
        out_shape=jax.ShapeDtypeStruct((points, xlen), f32),
        in_specs=[pl.BlockSpec(memory_space=pl.ANY)] * 8,
        out_specs=pl.BlockSpec(memory_space=pl.ANY),
        scratch_shapes=[
            pltpu.VMEM((blocks, points, LANES), f32),
            pltpu.VMEM((blocks, ylen, zlen, LANES), bf),
            pltpu.VMEM((blocks, points, LANES), f32),
            pltpu.VMEM((blocks, zlen, 2, ylen, LANES), bf),
            pltpu.VMEM((zlen, 2, ylen * rows, LANES), bf),
            pltpu.VMEM((zlen, ylen * rows, LANES), bf),
            pltpu.VMEM((blocks, zlen, ylen, LANES), bf),
            pltpu.VMEM((ylen, 2, zlen, xlen), bf),
            pltpu.VMEM((ylen, zlen, xlen), bf),
            pltpu.VMEM((yb, 2, zlen * cols, xlen), bf),
            pltpu.VMEM((yb, zlen * cols, xlen), bf),
            pltpu.VMEM((ylen, zlen, xlen), bf),
            *[pltpu.VMEM(m.shape, bf) for m in matrices],
            sems((2 * blocks + 8,)),
            sems((2 * (Y_CHUNKS + Z_CHUNKS),)),
            *[sems((Y_CHUNKS, rows - 1))] * 4,
            *[sems((Z_CHUNKS, cols - 1))] * 4,
        ],
        compiler_params=pltpu.CompilerParams(
            collective_id=0, has_side_effects=True, vmem_limit_bytes=56 * 1024 * 1024),
        cost_estimate=pl.CostEstimate(
            flops=flops, bytes_accessed=14 * points * xlen, transcendentals=0),
    )(scalars.reshape(points, xlen), velocity, *matrices)
    return result.reshape(scalars.shape)


def fits(rows, cols, shape):
    count, ylen, zlen, xlen = shape
    return (
        count == 1 and rows > 1 and cols > 1
        and xlen == LANES * rows
        and ylen % (16 * Z_CHUNKS) == 0 and ylen % (cols * Z_CHUNKS) == 0
        and zlen % 16 == 0 and zlen % Y_CHUNKS == 0
        and ylen * zlen * xlen <= 1 << 20
    )


def solution(mesh):
    rows, cols = mesh.shape["row"], mesh.shape["col"]

    def step(scalars, *rest):
        if fits(rows, cols, scalars.shape):
            return fused(rows, cols, scalars, *rest)
        return body(scalars, *rest)

    split = P(None, "row", "col", None)
    return jax.shard_map(
        step,
        mesh=mesh,
        in_specs=(split, split, P(), P(), P(), P(), P(), P()),
        out_specs=split,
        check_vma=False,
    )
```

```python
import functools

import jax
import jax.numpy as jnp
from jax import lax
from jax.experimental import pallas as pl
from jax.experimental.pallas import tpu as pltpu
from jax.sharding import PartitionSpec as P

diffusion_coefficient = 0.5
step_weight = 0.5
MESH = pl.DeviceIdType.MESH
LANES = 128

Y_CHUNKS = 8
Z_CHUNKS = 2


def contract_last(scalar_values, matrix):
    return lax.dot_general(
        scalar_values,
        matrix,
        (((scalar_values.ndim - 1,), (1,)), ((), ())),
        preferred_element_type=jnp.float32,
    )


def contract_middle(scalar_values, matrix):
    return jnp.einsum("syc,ky->skc", scalar_values, matrix, preferred_element_type=jnp.float32)


def derivative_pair(scalar_values, first_derivative_matrix, second_derivative_matrix, apply_matrix):
    return (
        apply_matrix(scalar_values, first_derivative_matrix),
        apply_matrix(scalar_values, second_derivative_matrix),
    )


def axis_contribution(
    scalar_values, velocity_field, first_derivative_matrix, second_derivative_matrix, apply_matrix
):
    velocity_flux = velocity_field.astype(jnp.float32)
    flux_product = (velocity_flux * scalar_values.astype(jnp.float32)).astype(jnp.bfloat16)
    scalar_gradient, second_derivative = derivative_pair(
        scalar_values, first_derivative_matrix, second_derivative_matrix, apply_matrix
    )
    advected_scalar = apply_matrix(flux_product, first_derivative_matrix)
    return (
        -0.5 * (velocity_flux * scalar_gradient + advected_scalar)
        + diffusion_coefficient * second_derivative
    )


def body(scalars, velocity, first_x, second_x, first_y, second_y, first_z, second_z):
    scalar_count = scalars.shape[0]
    rows_local = scalars.shape[1]
    depth_z = scalars.shape[2]
    length_x = scalars.shape[3]
    compiled_step = scalars.astype(jnp.bfloat16)
    x_term = axis_contribution(compiled_step, velocity[0], first_x, second_x, contract_last)
    turned = jnp.transpose(jnp.concatenate([compiled_step, velocity[1:]], axis=0), (0, 1, 3, 2))
    y_payload = turned[: scalar_count + 1].reshape(scalar_count + 1, rows_local, length_x * depth_z)
    z_payload = jnp.concatenate([turned[:scalar_count], turned[scalar_count + 1 :]], axis=0)
    pencil_y = lax.all_to_all(y_payload, "row", split_axis=2, concat_axis=1, tiled=True)
    pencil_z = lax.all_to_all(z_payload, "col", split_axis=2, concat_axis=3, tiled=True)
    y_term = axis_contribution(
        pencil_y[:scalar_count], pencil_y[scalar_count], first_y, second_y, contract_middle
    )
    z_term = axis_contribution(
        pencil_z[:scalar_count], pencil_z[scalar_count], first_z, second_z, contract_last
    )
    y_home = lax.all_to_all(y_term, "row", split_axis=1, concat_axis=2, tiled=True)
    z_home = lax.all_to_all(z_term, "col", split_axis=3, concat_axis=2, tiled=True)
    returned = y_home.reshape(scalar_count, rows_local, length_x, depth_z) + z_home
    returned = jnp.transpose(returned, (0, 1, 3, 2))
    return scalars + step_weight * (x_term + returned)


def pair_term(velocity, gradient, advected, second):
    half = 0.5 * step_weight
    return -half * (velocity * gradient + advected) + (step_weight * diffusion_coefficient) * second


def dot(a, b):
    return jnp.dot(a, b, preferred_element_type=jnp.float32)


def dot_rows(a, b):
    return lax.dot_general(a, b, (((1,), (1,)), ((), ())), preferred_element_type=jnp.float32)


def kernel(
    rows, cols, scal, vel, f1x, f2x, f1y, f2y, f1z, f2z, out,
    acc, vb, vf, turned, py, ysend, yhome, sw, ub, pz, zsend, zhome,
    m1x, m2x, m1y, m2y, m1z, m2z,
    in_sem, own_sem, yf_send, yf_recv, yr_send, yr_recv, zf_send, zf_recv, zr_send, zr_recv,
):
    my_row, my_col = lax.axis_index("row"), lax.axis_index("col")
    ylen, zlen, xlen = ub.shape
    blocks = xlen // LANES
    zc = zlen // Y_CHUNKS
    yb = ylen // cols
    yc = yb // Z_CHUNKS

    def row_of(d):
        return lax.rem(my_row + d, rows)

    def col_of(d):
        return lax.rem(my_col + d, cols)

    def lanes(b):
        return pl.ds(b * LANES, LANES)

    loads = []

    def load(src, dst):
        copy = pltpu.make_async_copy(src, dst, in_sem.at[len(loads)])
        copy.start()
        loads.append(copy)
        return copy

    scal_in = [load(scal.at[:, lanes(b)], acc.at[b]) for b in range(blocks)]
    v_in = [load(vel.at[1, :, :, lanes(b)], vb.at[b]) for b in range(blocks)]

    barrier = pltpu.get_barrier_semaphore()
    for d in range(1, rows):
        pl.semaphore_signal(barrier, inc=1, device_id=(row_of(d), my_col), device_id_type=MESH)
    for d in range(1, cols):
        pl.semaphore_signal(barrier, inc=1, device_id=(my_row, col_of(d)), device_id_type=MESH)

    def y_forward(k, part, d, sender, receiver):
        zs = pl.ds(k * zc, zc)
        return pltpu.make_async_remote_copy(
            src_ref=turned.at[part, receiver, zs],
            dst_ref=py.at[part, zs, pl.ds(sender * ylen, ylen)],
            send_sem=yf_send.at[k, part, d - 1], recv_sem=yf_recv.at[k, part, d - 1],
            device_id=(row_of(d), my_col), device_id_type=MESH)

    def y_return(k, d, sender, receiver):
        zs = pl.ds(k * zc, zc)
        return pltpu.make_async_remote_copy(
            src_ref=ysend.at[zs, pl.ds(receiver * ylen, ylen)],
            dst_ref=yhome.at[sender, zs],
            send_sem=yr_send.at[k, d - 1], recv_sem=yr_recv.at[k, d - 1],
            device_id=(row_of(d), my_col), device_id_type=MESH)

    def z_forward(k, d, sender, receiver):
        return pltpu.make_async_remote_copy(
            src_ref=sw.at[pl.ds(receiver * yb + k * yc, yc)],
            dst_ref=pz.at[pl.ds(k * yc, yc), :, pl.ds(sender * zlen, zlen)],
            send_sem=zf_send.at[k, d - 1], recv_sem=zf_recv.at[k, d - 1],
            device_id=(my_row, col_of(d)), device_id_type=MESH)

    def z_return(k, d, sender, receiver):
        return pltpu.make_async_remote_copy(
            src_ref=zsend.at[pl.ds(k * yc, yc), pl.ds(receiver * zlen, zlen)],
            dst_ref=zhome.at[pl.ds(sender * yb + k * yc, yc)],
            send_sem=zr_send.at[k, d - 1], recv_sem=zr_recv.at[k, d - 1],
            device_id=(my_row, col_of(d)), device_id_type=MESH)

    def own_copy(src, dst, index):
        copy = pltpu.make_async_copy(src, dst, own_sem.at[index])
        copy.start()
        return copy

    own = {}
    sends = []

    def order(n):
        return range(1, n)

    def turn_and_send_y(k, part):
        field = vf if part else acc

        @pl.loop(k * zc, (k + 1) * zc)
        def _(z):
            for b in range(blocks):
                turned[part, b, z] = field[b, pl.ds(z, ylen, stride=zlen), :].astype(jnp.bfloat16)

        if k == 0 and part == 0:
            pl.semaphore_wait(barrier, rows + cols - 2)
        for d in order(rows):
            copy = y_forward(k, part, d, my_row, row_of(d))
            copy.start()
            sends.append(copy)
        zs = pl.ds(k * zc, zc)
        own["yf", k, part] = own_copy(
            turned.at[part, my_row, zs], py.at[part, zs, pl.ds(my_row * ylen, ylen)], 2 * k + part)

    for copy in scal_in:
        copy.wait()
    turn_and_send_y(0, 0)
    w_in = load(vel.at[2], sw.at[:, 1])
    u_in = load(vel.at[0], ub)
    x_in = [load(f1x, m1x), load(f2x, m2x)]
    y_in = [load(f1y, m1y), load(f2y, m2y)]
    z_in = [load(f1z, m1z), load(f2z, m2z)]
    turn_and_send_y(1, 0)
    for copy in v_in:
        copy.wait()

    @pl.loop(0, ylen)
    def _(y):
        span = pl.ds(pl.multiple_of(y * zlen, zlen), zlen)
        for b in range(blocks):
            vf[b, span] = vb[b, y].astype(jnp.float32)

    turn_and_send_y(0, 1)
    turn_and_send_y(1, 1)

    @pl.loop(0, ylen)
    def _(y):
        span = pl.ds(pl.multiple_of(y * zlen, zlen), zlen)
        for b in range(blocks):
            sw[y, 0, :, lanes(b)] = acc[b, span].astype(jnp.bfloat16)

    w_in.wait()
    for k in range(Z_CHUNKS):
        for d in order(cols):
            copy = z_forward(k, d, my_col, col_of(d))
            copy.start()
            sends.append(copy)
        own["zf", k] = own_copy(
            sw.at[pl.ds(my_col * yb + k * yc, yc)],
            pz.at[pl.ds(k * yc, yc), :, pl.ds(my_col * zlen, zlen)], 2 * Y_CHUNKS + k)
    for k in range(2, Y_CHUNKS):
        for part in range(2):
            turn_and_send_y(k, part)

    u_in.wait()
    for copy in x_in:
        copy.wait()
    y_tile = max(1, 256 // zlen)
    while ylen % y_tile:
        y_tile -= 1
    tile = y_tile * zlen

    @pl.loop(0, ylen // y_tile)
    def _(i):
        ys = pl.ds(i * y_tile, y_tile)
        span = pl.ds(pl.multiple_of(i * tile, tile), tile)
        s = sw[ys, 0].reshape(tile, xlen)
        u = ub[ys].reshape(tile, xlen).astype(jnp.float32)
        flux = (u * s.astype(jnp.float32)).astype(jnp.bfloat16)
        term = pair_term(u, dot_rows(s, m1x[...]), dot_rows(flux, m1x[...]), dot_rows(s, m2x[...]))
        for b in range(blocks):
            acc[b, span] += term[:, b * LANES:(b + 1) * LANES]

    for copy in y_in + z_in:
        copy.wait()

    def y_terms(k):
        for part in range(2):
            own["yf", k, part].wait()
            for d in order(rows):
                y_forward(k, part, d, row_of(rows - d), my_row).wait_recv()

        @pl.loop(k * zc, (k + 1) * zc)
        def _(z):
            s = py[0, z]
            v = py[1, z].astype(jnp.float32)
            flux = (v * s.astype(jnp.float32)).astype(jnp.bfloat16)
            both = dot(m1y[...], jnp.concatenate([s, flux], axis=1))
            term = pair_term(v, both[:, :LANES], both[:, LANES:], dot(m2y[...], s))
            ysend[z] = term.astype(jnp.bfloat16)

        for d in order(rows):
            copy = y_return(k, d, my_row, row_of(d))
            copy.start()
            sends.append(copy)
        zs = pl.ds(k * zc, zc)
        own["yr", k] = own_copy(
            ysend.at[zs, pl.ds(my_row * ylen, ylen)], yhome.at[my_row, zs],
            2 * Y_CHUNKS + Z_CHUNKS + k)

    def z_terms(k):
        own["zf", k].wait()
        for d in order(cols):
            z_forward(k, d, col_of(cols - d), my_col).wait_recv()

        @pl.loop(k * yc, (k + 1) * yc)
        def _(y):
            s = pz[y, 0]
            w = pz[y, 1].astype(jnp.float32)
            flux = (w * s.astype(jnp.float32)).astype(jnp.bfloat16)
            term = pair_term(w, dot(m1z[...], s), dot(m1z[...], flux), dot(m2z[...], s))
            zsend[y] = term.astype(jnp.bfloat16)

        for d in order(cols):
            copy = z_return(k, d, my_col, col_of(d))
            copy.start()
            sends.append(copy)
        own["zr", k] = own_copy(
            zsend.at[pl.ds(k * yc, yc), pl.ds(my_col * zlen, zlen)],
            zhome.at[pl.ds(my_col * yb + k * yc, yc)],
            3 * Y_CHUNKS + Z_CHUNKS + k)

    y_terms(0)
    for k in range(Z_CHUNKS):
        z_terms(k)
    for k in range(1, Y_CHUNKS):
        y_terms(k)

    for k in range(Z_CHUNKS):
        own["zr", k].wait()
        for d in order(cols):
            z_return(k, d, col_of(cols - d), my_col).wait_recv()

    @pl.loop(0, ylen)
    def _(y):
        span = pl.ds(pl.multiple_of(y * zlen, zlen), zlen)
        for b in range(blocks):
            acc[b, span] += zhome[y, :, lanes(b)].astype(jnp.float32)

    for k in range(Y_CHUNKS):
        own["yr", k].wait()
        for d in order(rows):
            y_return(k, d, row_of(rows - d), my_row).wait_recv()

        @pl.loop(k * zc, (k + 1) * zc)
        def _(z):
            for b in range(blocks):
                span = pl.ds(z, ylen, stride=zlen)
                acc[b, span, :] = acc[b, span, :] + yhome[b, z].astype(jnp.float32)

    stores = []
    for b in range(blocks):
        copy = pltpu.make_async_copy(acc.at[b], out.at[:, lanes(b)], in_sem.at[b])
        copy.start()
        stores.append(copy)
    for copy in sends:
        copy.wait_send()
    for copy in stores:
        copy.wait()


def fused(rows, cols, scalars, velocity, *matrices):
    _, ylen, zlen, xlen = scalars.shape
    blocks = xlen // LANES
    points = ylen * zlen
    yb = ylen // cols
    bf, f32 = jnp.bfloat16, jnp.float32
    sems = pltpu.SemaphoreType.DMA
    flops = 6 * points * xlen * (xlen + ylen * rows + zlen * cols)
    result = pl.pallas_call(
        functools.partial(kernel, rows, cols),
        out_shape=jax.ShapeDtypeStruct((points, xlen), f32),
        in_specs=[pl.BlockSpec(memory_space=pl.ANY)] * 8,
        out_specs=pl.BlockSpec(memory_space=pl.ANY),
        scratch_shapes=[
            pltpu.VMEM((blocks, points, LANES), f32),
            pltpu.VMEM((blocks, ylen, zlen, LANES), bf),
            pltpu.VMEM((blocks, points, LANES), f32),
            pltpu.VMEM((2, blocks, zlen, ylen, LANES), bf),
            pltpu.VMEM((2, zlen, ylen * rows, LANES), bf),
            pltpu.VMEM((zlen, ylen * rows, LANES), bf),
            pltpu.VMEM((blocks, zlen, ylen, LANES), bf),
            pltpu.VMEM((ylen, 2, zlen, xlen), bf),
            pltpu.VMEM((ylen, zlen, xlen), bf),
            pltpu.VMEM((yb, 2, zlen * cols, xlen), bf),
            pltpu.VMEM((yb, zlen * cols, xlen), bf),
            pltpu.VMEM((ylen, zlen, xlen), bf),
            *[pltpu.VMEM(m.shape, bf) for m in matrices],
            sems((2 * blocks + 8,)),
            sems((3 * Y_CHUNKS + 2 * Z_CHUNKS,)),
            *[sems((Y_CHUNKS, 2, rows - 1))] * 2,
            *[sems((Y_CHUNKS, rows - 1))] * 2,
            *[sems((Z_CHUNKS, cols - 1))] * 4,
        ],
        compiler_params=pltpu.CompilerParams(
            collective_id=0, has_side_effects=True, vmem_limit_bytes=47 * 1024 * 1024),
        cost_estimate=pl.CostEstimate(
            flops=flops, bytes_accessed=14 * points * xlen, transcendentals=0),
    )(scalars.reshape(points, xlen), velocity,
      *[pltpu.with_memory_space_constraint(m, pltpu.HBM) for m in matrices])
    return result.reshape(scalars.shape)


def fits(rows, cols, shape):
    count, ylen, zlen, xlen = shape
    return (
        count == 1 and rows > 1 and cols > 1
        and xlen == LANES * rows
        and Y_CHUNKS > 1 and ylen % 16 == 0 and ylen % (cols * Z_CHUNKS) == 0
        and zlen % 16 == 0 and zlen % Y_CHUNKS == 0
        and ylen * zlen * xlen <= 1 << 20
    )


def solution(mesh):
    rows, cols = mesh.shape["row"], mesh.shape["col"]

    def step(scalars, *rest):
        if fits(rows, cols, scalars.shape):
            return fused(rows, cols, scalars, *rest)
        return body(scalars, *rest)

    split = P(None, "row", "col", None)
    return jax.shard_map(
        step,
        mesh=mesh,
        in_specs=(split, split, P(), P(), P(), P(), P(), P()),
        out_specs=split,
        check_vma=False,
    )
```

```python
import functools

import jax
import jax.numpy as jnp
from jax import lax
from jax.experimental import pallas as pl
from jax.experimental.pallas import tpu as pltpu
from jax.sharding import PartitionSpec as P

diffusion_coefficient = 0.5
step_weight = 0.5
MESH = pl.DeviceIdType.MESH
LANES = 128

Y_CHUNKS = 8
Z_CHUNKS = 2


def contract_last(scalar_values, matrix):
    return lax.dot_general(
        scalar_values,
        matrix,
        (((scalar_values.ndim - 1,), (1,)), ((), ())),
        preferred_element_type=jnp.float32,
    )


def contract_middle(scalar_values, matrix):
    return jnp.einsum("syc,ky->skc", scalar_values, matrix, preferred_element_type=jnp.float32)


def derivative_pair(scalar_values, first_derivative_matrix, second_derivative_matrix, apply_matrix):
    return (
        apply_matrix(scalar_values, first_derivative_matrix),
        apply_matrix(scalar_values, second_derivative_matrix),
    )


def axis_contribution(
    scalar_values, velocity_field, first_derivative_matrix, second_derivative_matrix, apply_matrix
):
    velocity_flux = velocity_field.astype(jnp.float32)
    flux_product = (velocity_flux * scalar_values.astype(jnp.float32)).astype(jnp.bfloat16)
    scalar_gradient, second_derivative = derivative_pair(
        scalar_values, first_derivative_matrix, second_derivative_matrix, apply_matrix
    )
    advected_scalar = apply_matrix(flux_product, first_derivative_matrix)
    return (
        -0.5 * (velocity_flux * scalar_gradient + advected_scalar)
        + diffusion_coefficient * second_derivative
    )


def body(scalars, velocity, first_x, second_x, first_y, second_y, first_z, second_z):
    scalar_count = scalars.shape[0]
    rows_local = scalars.shape[1]
    depth_z = scalars.shape[2]
    length_x = scalars.shape[3]
    compiled_step = scalars.astype(jnp.bfloat16)
    x_term = axis_contribution(compiled_step, velocity[0], first_x, second_x, contract_last)
    turned = jnp.transpose(jnp.concatenate([compiled_step, velocity[1:]], axis=0), (0, 1, 3, 2))
    y_payload = turned[: scalar_count + 1].reshape(scalar_count + 1, rows_local, length_x * depth_z)
    z_payload = jnp.concatenate([turned[:scalar_count], turned[scalar_count + 1 :]], axis=0)
    pencil_y = lax.all_to_all(y_payload, "row", split_axis=2, concat_axis=1, tiled=True)
    pencil_z = lax.all_to_all(z_payload, "col", split_axis=2, concat_axis=3, tiled=True)
    y_term = axis_contribution(
        pencil_y[:scalar_count], pencil_y[scalar_count], first_y, second_y, contract_middle
    )
    z_term = axis_contribution(
        pencil_z[:scalar_count], pencil_z[scalar_count], first_z, second_z, contract_last
    )
    y_home = lax.all_to_all(y_term, "row", split_axis=1, concat_axis=2, tiled=True)
    z_home = lax.all_to_all(z_term, "col", split_axis=3, concat_axis=2, tiled=True)
    returned = y_home.reshape(scalar_count, rows_local, length_x, depth_z) + z_home
    returned = jnp.transpose(returned, (0, 1, 3, 2))
    return scalars + step_weight * (x_term + returned)


def pair_term(velocity, gradient, advected, second):
    half = 0.5 * step_weight
    return -half * (velocity * gradient + advected) + (step_weight * diffusion_coefficient) * second


def dot(a, b):
    return jnp.dot(a, b, preferred_element_type=jnp.float32)


def dot_rows(a, b):
    return lax.dot_general(a, b, (((1,), (1,)), ((), ())), preferred_element_type=jnp.float32)


def kernel(
    rows, cols, scal, vel, f1x, f2x, f1y, f2y, f1z, f2z, out,
    acc, vb, vf, turned, py, ysend, yhome, sw, ub, pz, zsend, zhome,
    m1x, m2x, m1y, m2y, m1z, m2z,
    in_sem, own_sem, yf_send, yf_recv, yr_send, yr_recv, zf_send, zf_recv, zr_send, zr_recv,
):
    my_row, my_col = lax.axis_index("row"), lax.axis_index("col")
    ylen, zlen, xlen = ub.shape
    blocks = xlen // LANES
    zc = zlen // Y_CHUNKS
    yb = ylen // cols
    yc = yb // Z_CHUNKS

    def row_of(d):
        return lax.rem(my_row + d, rows)

    def col_of(d):
        return lax.rem(my_col + d, cols)

    def lanes(b):
        return pl.ds(b * LANES, LANES)

    loads = []

    def load(src, dst):
        copy = pltpu.make_async_copy(src, dst, in_sem.at[len(loads)])
        copy.start()
        loads.append(copy)
        return copy

    scal_in = [load(scal.at[:, lanes(b)], acc.at[b]) for b in range(blocks)]
    v_in = [load(vel.at[1, :, :, lanes(b)], vb.at[b]) for b in range(blocks)]

    barrier = pltpu.get_barrier_semaphore()
    for d in range(1, rows):
        pl.semaphore_signal(barrier, inc=1, device_id=(row_of(d), my_col), device_id_type=MESH)
    for d in range(1, cols):
        pl.semaphore_signal(barrier, inc=1, device_id=(my_row, col_of(d)), device_id_type=MESH)

    def y_forward(k, part, d, sender, receiver):
        zs = pl.ds(k * zc, zc)
        return pltpu.make_async_remote_copy(
            src_ref=turned.at[part, receiver, zs],
            dst_ref=py.at[part, zs, pl.ds(sender * ylen, ylen)],
            send_sem=yf_send.at[k, part, d - 1], recv_sem=yf_recv.at[k, part, d - 1],
            device_id=(row_of(d), my_col), device_id_type=MESH)

    def y_return(k, d, sender, receiver):
        zs = pl.ds(k * zc, zc)
        return pltpu.make_async_remote_copy(
            src_ref=ysend.at[zs, pl.ds(receiver * ylen, ylen)],
            dst_ref=yhome.at[sender, zs],
            send_sem=yr_send.at[k, d - 1], recv_sem=yr_recv.at[k, d - 1],
            device_id=(row_of(d), my_col), device_id_type=MESH)

    def z_forward(k, d, sender, receiver):
        return pltpu.make_async_remote_copy(
            src_ref=sw.at[pl.ds(receiver * yb + k * yc, yc)],
            dst_ref=pz.at[pl.ds(k * yc, yc), :, pl.ds(sender * zlen, zlen)],
            send_sem=zf_send.at[k, d - 1], recv_sem=zf_recv.at[k, d - 1],
            device_id=(my_row, col_of(d)), device_id_type=MESH)

    def z_return(k, d, sender, receiver):
        return pltpu.make_async_remote_copy(
            src_ref=zsend.at[pl.ds(k * yc, yc), pl.ds(receiver * zlen, zlen)],
            dst_ref=zhome.at[pl.ds(sender * yb + k * yc, yc)],
            send_sem=zr_send.at[k, d - 1], recv_sem=zr_recv.at[k, d - 1],
            device_id=(my_row, col_of(d)), device_id_type=MESH)

    def own_copy(src, dst, index):
        copy = pltpu.make_async_copy(src, dst, own_sem.at[index])
        copy.start()
        return copy

    own = {}
    sends = []

    def order(n):
        return range(1, n)

    def turn_and_send_y(k, part):
        field = vf if part else acc

        @pl.loop(k * zc, (k + 1) * zc)
        def _(z):
            for b in range(blocks):
                turned[part, b, z] = field[b, pl.ds(z, ylen, stride=zlen), :].astype(jnp.bfloat16)

        if k == 0 and part == 0:
            pl.semaphore_wait(barrier, rows + cols - 2)
        for d in order(rows):
            copy = y_forward(k, part, d, my_row, row_of(d))
            copy.start()
            sends.append(copy)
        zs = pl.ds(k * zc, zc)
        own["yf", k, part] = own_copy(
            turned.at[part, my_row, zs], py.at[part, zs, pl.ds(my_row * ylen, ylen)], 2 * k + part)

    for copy in scal_in:
        copy.wait()
    turn_and_send_y(0, 0)
    w_in = load(vel.at[2], sw.at[:, 1])
    u_in = load(vel.at[0], ub)
    x_in = [load(f1x, m1x), load(f2x, m2x)]
    y_in = [load(f1y, m1y), load(f2y, m2y)]
    z_in = [load(f1z, m1z), load(f2z, m2z)]
    turn_and_send_y(1, 0)
    for copy in v_in:
        copy.wait()

    @pl.loop(0, ylen)
    def _(y):
        span = pl.ds(pl.multiple_of(y * zlen, zlen), zlen)
        for b in range(blocks):
            vf[b, span] = vb[b, y].astype(jnp.float32)

    turn_and_send_y(0, 1)
    turn_and_send_y(1, 1)

    @pl.loop(0, ylen)
    def _(y):
        span = pl.ds(pl.multiple_of(y * zlen, zlen), zlen)
        for b in range(blocks):
            sw[y, 0, :, lanes(b)] = acc[b, span].astype(jnp.bfloat16)

    w_in.wait()
    for k in range(Z_CHUNKS):
        for d in order(cols):
            copy = z_forward(k, d, my_col, col_of(d))
            copy.start()
            sends.append(copy)
        own["zf", k] = own_copy(
            sw.at[pl.ds(my_col * yb + k * yc, yc)],
            pz.at[pl.ds(k * yc, yc), :, pl.ds(my_col * zlen, zlen)], 2 * Y_CHUNKS + k)
    for k in range(2, Y_CHUNKS):
        for part in range(2):
            turn_and_send_y(k, part)

    u_in.wait()
    for copy in x_in:
        copy.wait()
    y_tile = max(1, 256 // zlen)
    while ylen % y_tile:
        y_tile -= 1
    tile = y_tile * zlen

    @pl.loop(0, ylen // y_tile)
    def _(i):
        ys = pl.ds(i * y_tile, y_tile)
        span = pl.ds(pl.multiple_of(i * tile, tile), tile)
        s = sw[ys, 0].reshape(tile, xlen)
        u = ub[ys].reshape(tile, xlen).astype(jnp.float32)
        flux = (u * s.astype(jnp.float32)).astype(jnp.bfloat16)
        term = pair_term(u, dot_rows(s, m1x[...]), dot_rows(flux, m1x[...]), dot_rows(s, m2x[...]))
        for b in range(blocks):
            acc[b, span] += term[:, b * LANES:(b + 1) * LANES]

    for copy in y_in + z_in:
        copy.wait()

    def y_terms(k):
        for part in range(2):
            own["yf", k, part].wait()
            for d in order(rows):
                y_forward(k, part, d, row_of(rows - d), my_row).wait_recv()

        @pl.loop(k * zc, (k + 1) * zc)
        def _(z):
            s = py[0, z]
            v = py[1, z].astype(jnp.float32)
            flux = (v * s.astype(jnp.float32)).astype(jnp.bfloat16)
            both = dot(m1y[...], jnp.concatenate([s, flux], axis=1))
            term = pair_term(v, both[:, :LANES], both[:, LANES:], dot(m2y[...], s))
            ysend[z] = term.astype(jnp.bfloat16)

        for d in order(rows):
            copy = y_return(k, d, my_row, row_of(d))
            copy.start()
            sends.append(copy)
        zs = pl.ds(k * zc, zc)
        own["yr", k] = own_copy(
            ysend.at[zs, pl.ds(my_row * ylen, ylen)], yhome.at[my_row, zs],
            2 * Y_CHUNKS + Z_CHUNKS + k)

    def z_terms(k):
        own["zf", k].wait()
        for d in order(cols):
            z_forward(k, d, col_of(cols - d), my_col).wait_recv()

        @pl.loop(k * yc, (k + 1) * yc)
        def _(y):
            s = pz[y, 0]
            w = pz[y, 1].astype(jnp.float32)
            flux = (w * s.astype(jnp.float32)).astype(jnp.bfloat16)
            term = pair_term(w, dot(m1z[...], s), dot(m1z[...], flux), dot(m2z[...], s))
            zsend[y] = term.astype(jnp.bfloat16)

        for d in order(cols):
            copy = z_return(k, d, my_col, col_of(d))
            copy.start()
            sends.append(copy)
        own["zr", k] = own_copy(
            zsend.at[pl.ds(k * yc, yc), pl.ds(my_col * zlen, zlen)],
            zhome.at[pl.ds(my_col * yb + k * yc, yc)],
            3 * Y_CHUNKS + Z_CHUNKS + k)

    y_terms(0)
    for k in range(Z_CHUNKS):
        z_terms(k)
    for k in range(1, Y_CHUNKS):
        y_terms(k)

    for k in range(Z_CHUNKS):
        own["zr", k].wait()
        for d in order(cols):
            z_return(k, d, col_of(cols - d), my_col).wait_recv()

    @pl.loop(0, ylen)
    def _(y):
        span = pl.ds(pl.multiple_of(y * zlen, zlen), zlen)
        for b in range(blocks):
            acc[b, span] += zhome[y, :, lanes(b)].astype(jnp.float32)

    stores = []
    for k in range(Y_CHUNKS):
        for d in range(rows):
            sender = row_of(rows - d)
            if d == 0:
                own["yr", k].wait()
            else:
                y_return(k, d, sender, my_row).wait_recv()

            @pl.loop(k * zc, (k + 1) * zc)
            def _(z):
                span = pl.ds(z, ylen, stride=zlen)
                acc[sender, span, :] = acc[sender, span, :] + yhome[sender, z].astype(jnp.float32)

            if k == Y_CHUNKS - 1:
                block = pl.ds(pl.multiple_of(sender * LANES, LANES), LANES)
                copy = pltpu.make_async_copy(acc.at[sender], out.at[:, block], in_sem.at[d])
                copy.start()
                stores.append(copy)

    for copy in sends:
        copy.wait_send()
    for copy in stores:
        copy.wait()


def fused(rows, cols, scalars, velocity, *matrices):
    _, ylen, zlen, xlen = scalars.shape
    blocks = xlen // LANES
    points = ylen * zlen
    yb = ylen // cols
    bf, f32 = jnp.bfloat16, jnp.float32
    sems = pltpu.SemaphoreType.DMA
    flops = 6 * points * xlen * (xlen + ylen * rows + zlen * cols)
    result = pl.pallas_call(
        functools.partial(kernel, rows, cols),
        out_shape=jax.ShapeDtypeStruct((points, xlen), f32),
        in_specs=[pl.BlockSpec(memory_space=pl.ANY)] * 8,
        out_specs=pl.BlockSpec(memory_space=pl.ANY),
        scratch_shapes=[
            pltpu.VMEM((blocks, points, LANES), f32),
            pltpu.VMEM((blocks, ylen, zlen, LANES), bf),
            pltpu.VMEM((blocks, points, LANES), f32),
            pltpu.VMEM((2, blocks, zlen, ylen, LANES), bf),
            pltpu.VMEM((2, zlen, ylen * rows, LANES), bf),
            pltpu.VMEM((zlen, ylen * rows, LANES), bf),
            pltpu.VMEM((blocks, zlen, ylen, LANES), bf),
            pltpu.VMEM((ylen, 2, zlen, xlen), bf),
            pltpu.VMEM((ylen, zlen, xlen), bf),
            pltpu.VMEM((yb, 2, zlen * cols, xlen), bf),
            pltpu.VMEM((yb, zlen * cols, xlen), bf),
            pltpu.VMEM((ylen, zlen, xlen), bf),
            *[pltpu.VMEM(m.shape, bf) for m in matrices],
            sems((2 * blocks + 8,)),
            sems((3 * Y_CHUNKS + 2 * Z_CHUNKS,)),
            *[sems((Y_CHUNKS, 2, rows - 1))] * 2,
            *[sems((Y_CHUNKS, rows - 1))] * 2,
            *[sems((Z_CHUNKS, cols - 1))] * 4,
        ],
        compiler_params=pltpu.CompilerParams(
            collective_id=0, has_side_effects=True, vmem_limit_bytes=47 * 1024 * 1024),
        cost_estimate=pl.CostEstimate(
            flops=flops, bytes_accessed=14 * points * xlen, transcendentals=0),
    )(scalars.reshape(points, xlen), velocity,
      *[pltpu.with_memory_space_constraint(m, pltpu.HBM) for m in matrices])
    return result.reshape(scalars.shape)


def fits(rows, cols, shape):
    count, ylen, zlen, xlen = shape
    return (
        count == 1 and rows > 1 and cols > 1
        and xlen == LANES * rows
        and Y_CHUNKS > 1 and ylen % 16 == 0 and ylen % (cols * Z_CHUNKS) == 0
        and zlen % 16 == 0 and zlen % Y_CHUNKS == 0
        and ylen * zlen * xlen <= 1 << 20
    )


def solution(mesh):
    rows, cols = mesh.shape["row"], mesh.shape["col"]

    def step(scalars, *rest):
        if fits(rows, cols, scalars.shape):
            return fused(rows, cols, scalars, *rest)
        return body(scalars, *rest)

    split = P(None, "row", "col", None)
    return jax.shard_map(
        step,
        mesh=mesh,
        in_specs=(split, split, P(), P(), P(), P(), P(), P()),
        out_specs=split,
        check_vma=False,
    )
```
